512 devices in a mesh: dp: 16 (over z_lo, core), seq: 32 (over y, x, z_hi).
Axes of the slice: x: 4, y: 4, z: 16 (z_hi: 2, z_lo: 8; z = z_hi * 8 + z_lo), core: 2. Of those that a mesh axis runs over, the one named last changes fastest.
Arguments:
- queries: bfloat16 [16, 4096, 2048], P('dp', 'seq'), may hold values from -40 to 40, as said below
- keys: bfloat16 [16, 4096, 2048], P('dp', 'seq'), may hold values from -10 to 10, as said below
- values: bfloat16 [16, 4096, 2048], P('dp', 'seq'), may hold values from -6 to 6
- position_keys: bfloat16 [384, 2048], P('dp'), may hold values from -6 to 6
- content_bias: bfloat16 [2048], P('dp'), may hold values from -3 to 3
- position_bias: bfloat16 [2048], P('dp'), may hold values from -3 to 3
- out_grad: bfloat16 [16, 4096, 2048], P('dp', 'seq'), may hold values from -6 to 6
Outputs:
- attended: bfloat16 [16, 4096, 2048], P('dp', 'seq')
- query_grad: bfloat16 [16, 4096, 2048], P('dp', 'seq')
- key_grad: bfloat16 [16, 4096, 2048], P('dp', 'seq')
- value_grad: bfloat16 [16, 4096, 2048], P('dp', 'seq')
- position_key_grad: float32 [384, 2048], P('dp')
- content_grad: float32 [2048], P('dp')
- position_grad: float32 [2048], P('dp')
The draws below stay inside these ranges and needn't reach their ends.
Inputs may be any that keep to these rules, and one draw needn't show every extreme that they name: `queries`: entries bounded. `keys`: entries bounded.
All inputs are finite; a program needn't handle non-finite values.
Results may differ from the reference program's by a relative error of at most 0.0098.
Values may be sent and summed in bfloat16 or wider, within the bound.
A program may use at most 128 MiB of HBM per device.

```python
import jax
import jax.numpy as jnp
from jax import lax

H = 16
HEAD = 128
SEG = 128
MEM = 256
HD = 2048
REL = 384
STREAMS = 16
TOKENS = 4096
N_SEQ = 32


def draw_queries(key, part):
    key = jax.random.fold_in(key, 1)
    fresh = jnp.clip(jax.random.normal(key, (STREAMS, TOKENS, HD), jnp.float32), -4.0, 4.0)
    return fresh.astype(jnp.bfloat16)


def draw_keys(key, part):
    key = jax.random.fold_in(key, 2)
    fresh = jnp.clip(jax.random.normal(key, (STREAMS, TOKENS, HD), jnp.float32), -4.0, 4.0)
    return fresh.astype(jnp.bfloat16)


def block_levels(own_key, extent, pieces, smallest, top_value):
    def one(position, blocks):
        heights = jax.random.uniform(jax.random.fold_in(jax.random.fold_in(own_key, 6), position), (blocks,), jnp.float32, smallest / len(pieces), top_value / len(pieces))
        return jnp.repeat(jnp.exp(heights), extent[position] // blocks).reshape((-1,) + (1,) * (len(extent) - position - 1))

    loudness = one(*pieces[0])
    for cut in pieces[1:]:
        loudness = loudness * one(*cut)
    return loudness


def gaussian(rng, dims, width, bound, split=(), kind=jnp.bfloat16):
    level = block_levels(rng, dims, split, -0.22, 0.18) if split else 1.0
    array = jax.random.normal(rng, dims, jnp.float32) * width * level
    return jnp.minimum(jnp.maximum(array, -bound), bound).astype(kind)


def setup_inputs(seed: int = 0) -> dict:
    key_list = jax.random.split(jax.random.key(seed), 8)
    queries = draw_queries(jax.random.fold_in(key_list[7], 71), 0)
    keys = draw_keys(jax.random.fold_in(key_list[7], 71), 0)
    values = gaussian(key_list[2], (STREAMS, TOKENS, HD), 1.0, 6.0, ((0, 16), (1, 32)))
    position_keys = gaussian(key_list[3], (REL, HD), 1.0, 6.0, ((0, 16),))
    content_bias = gaussian(key_list[4], (HD,), 0.5, 3.0, ((0, 16),))
    position_bias = gaussian(key_list[5], (HD,), 0.5, 3.0, ((0, 16),))
    out_grad = gaussian(key_list[6], (STREAMS, TOKENS, HD), 1.0, 6.0, ((0, 16), (1, 32)))
    return {"queries": queries, "keys": keys, "values": values, "position_keys": position_keys, "content_bias": content_bias, "position_bias": position_bias, "out_grad": out_grad}


def segment_pass(query_rows, key_rows, value_rows, grad_rows, table_rows, content_bias, position_bias, segment):
    factor = HEAD ** -0.5
    query_float = query_rows.astype(jnp.float32)
    content_query = (query_float + content_bias.astype(jnp.float32)).astype(jnp.bfloat16)
    position_query = (query_float + position_bias.astype(jnp.float32)).astype(jnp.bfloat16)
    content_heads = content_query.reshape(SEG, H, HEAD).astype(jnp.float32)
    position_heads = position_query.reshape(SEG, H, HEAD).astype(jnp.float32)
    key_heads = key_rows.reshape(REL, H, HEAD).astype(jnp.float32)
    value_heads = value_rows.reshape(REL, H, HEAD).astype(jnp.float32)
    table_heads = table_rows.reshape(REL, H, HEAD).astype(jnp.float32)
    grad_heads = grad_rows.reshape(SEG, H, HEAD).astype(jnp.float32)
    content_scores = jnp.einsum("ihd,jhd->hij", content_heads, key_heads)
    table_scores = jnp.einsum("ihd,rhd->hir", position_heads, table_heads)
    query_index = jnp.arange(SEG, dtype=jnp.int32)[:, None]
    column_index = jnp.arange(REL, dtype=jnp.int32)[None, :]
    distance = MEM + query_index - column_index
    allowed = (distance >= 0) & (segment * SEG - MEM + column_index >= 0)
    gather_at = jnp.broadcast_to(jnp.maximum(distance, 0)[None], (H, SEG, REL))
    positional = jnp.take_along_axis(table_scores, gather_at, axis=2)
    scores = (content_scores + positional) * factor
    highest = jnp.max(jnp.where(allowed[None], scores, -1e30), axis=-1, keepdims=True)
    raised = jnp.exp(jnp.where(allowed[None], scores - highest, -1e30))
    weights = raised / jnp.sum(raised, axis=-1, keepdims=True)
    rounded_weights = weights.astype(jnp.bfloat16)
    weight_float = rounded_weights.astype(jnp.float32)
    attended = jnp.einsum("hij,jhd->ihd", weight_float, value_heads).reshape(SEG, HD).astype(jnp.bfloat16)
    grad_probs = jnp.einsum("ihd,jhd->hij", grad_heads, value_heads)
    weighted_mean = jnp.sum(weights * grad_probs, axis=-1, keepdims=True)
    grad_scores = (weights * (grad_probs - weighted_mean) * factor).astype(jnp.bfloat16)
    key_at = MEM + query_index - column_index
    in_range = (key_at >= 0) & (key_at < REL)
    pick_at = jnp.broadcast_to(jnp.clip(key_at, 0, REL - 1)[None], (H, SEG, REL))
    grad_table = jnp.where(in_range[None], jnp.take_along_axis(grad_scores, pick_at, axis=2), jnp.zeros((), jnp.bfloat16))
    score_float = grad_scores.astype(jnp.float32)
    table_float = grad_table.astype(jnp.float32)
    grad_content = jnp.einsum("hij,jhd->ihd", score_float, key_heads)
    grad_position = jnp.einsum("hir,rhd->ihd", table_float, table_heads)
    query_grad = (grad_content + grad_position).reshape(SEG, HD).astype(jnp.bfloat16)
    key_part = jnp.einsum("hij,ihd->jhd", score_float, content_heads).reshape(REL, HD)
    value_part = jnp.einsum("hij,ihd->jhd", weight_float, grad_heads).reshape(REL, HD)
    table_grad = jnp.einsum("hir,ihd->rhd", table_float, position_heads).reshape(REL, HD)
    content_part = jnp.sum(grad_content.reshape(SEG, HD), axis=0)
    position_part = jnp.sum(grad_position.reshape(SEG, HD), axis=0)
    return attended, query_grad, key_part, value_part, table_grad, content_part, position_part


def spread_back(parts):
    piece_rows = min(SEG, MEM)
    reach_count = MEM // piece_rows
    own_part = parts[:, MEM:]
    memory_part = parts[:, :MEM].reshape(N_SEQ, reach_count, piece_rows, HD)
    for offset in range(reach_count):
        hops_back = reach_count - offset
        moved = jnp.concatenate([memory_part[hops_back:, offset], jnp.zeros((hops_back, piece_rows, HD), jnp.float32)], axis=0)
        own_part = own_part.at[:, SEG - piece_rows:].add(moved)
    return own_part.reshape(TOKENS, HD).astype(jnp.bfloat16)


def reference(queries, keys, values, position_keys, content_bias, position_bias, out_grad):
    def one_stream(stream):
        query_stream, key_stream, value_stream, grad_stream = stream
        padded_keys = jnp.concatenate([jnp.zeros((MEM, HD), jnp.bfloat16), key_stream], axis=0)
        padded_values = jnp.concatenate([jnp.zeros((MEM, HD), jnp.bfloat16), value_stream], axis=0)

        def one_segment(segment):
            start = (segment * SEG).astype(jnp.int32)
            query_rows = lax.dynamic_slice_in_dim(query_stream, start, SEG, 0)
            grad_rows = lax.dynamic_slice_in_dim(grad_stream, start, SEG, 0)
            key_rows = lax.dynamic_slice_in_dim(padded_keys, start, REL, 0)
            value_rows = lax.dynamic_slice_in_dim(padded_values, start, REL, 0)
            return segment_pass(query_rows, key_rows, value_rows, grad_rows, position_keys, content_bias, position_bias, segment)

        results = lax.map(one_segment, jnp.arange(N_SEQ, dtype=jnp.int32))
        return (results[0].reshape(TOKENS, HD), results[1].reshape(TOKENS, HD), spread_back(results[2]), spread_back(results[3]), jnp.sum(results[4], axis=0), jnp.sum(results[5], axis=0), jnp.sum(results[6], axis=0))

    outcome = lax.map(one_stream, (queries, keys, values, out_grad))
    return (outcome[0], outcome[1], outcome[2], outcome[3], jnp.sum(outcome[4], axis=0), jnp.sum(outcome[5], axis=0), jnp.sum(outcome[6], axis=0))
```

```python
import functools

import jax
import jax.numpy as jnp
from jax import lax
from jax.experimental import pallas as pl
from jax.experimental.pallas import tpu as pltpu
from jax.sharding import PartitionSpec as P

H = 16
HEAD = 128
SEG = 128
MEM = 256
HD = 2048
REL = 384
DP = 16
NZ = 8
PLANE = 16
ROWS = REL // DP
MSG = 32
TGRAD = REL + 16
PARTNERS = (PLANE - 1) + (NZ - 1) + 1 + 2

F32 = jnp.float32
BF16 = jnp.bfloat16


def dot_nt(a, b):
    return lax.dot_general(a, b, (((1,), (1,)), ((), ())), preferred_element_type=F32)


def dot_nn(a, b):
    return lax.dot_general(a, b, (((1,), (0,)), ((), ())), preferred_element_type=F32)


def dot_tn(a, b):
    return lax.dot_general(a, b, (((0,), (0,)), ((), ())), preferred_element_type=F32)


def columns(head):
    return pl.ds(pl.multiple_of(head * HEAD, HEAD), HEAD)


def kernel(
    q_hbm, k_hbm, v_hbm, g_hbm, table_ref, ub_ref, vb_ref,
    att_ref, qg_ref, kg_ref, vg_ref, tg_ref, cg_ref, pg_ref,
    q_buf, g_buf, k_buf, v_buf, own_k, own_v, back_k, back_v, got_k, got_v,
    msg_f, tz, flat, table, tgrad_out, tgrad_in, parts, sib_in, half_in, pair_out, pair_in, fin,
    local_sem, own_sem, halo_s, halo_r, ret_s, ret_r, tz_s, tz_r, sib_s, sib_r,
    tab_s, tab_r, tg_s, tg_r, half_s, half_r, pair_s, pair_r, fin_s, fin_r,
):
    dp = lax.axis_index("dp")
    seq = lax.axis_index("seq")
    zl = dp // 2
    core = dp % 2
    other = 1 - core
    plane = seq // 2
    zh = seq % 2

    def remote(src, dst, ss, rs, to_dp, to_seq):
        return pltpu.make_async_remote_copy(
            src_ref=src, dst_ref=dst, send_sem=ss, recv_sem=rs,
            device_id={"dp": to_dp, "seq": to_seq}, device_id_type=pl.DeviceIdType.MESH,
        )

    def seq_at(step):
        return (seq + step + 32) % 32

    def plane_seq(p):
        return p * 2 + zh

    load_q = pltpu.make_async_copy(q_hbm, q_buf, local_sem.at[0])
    load_g = pltpu.make_async_copy(g_hbm, g_buf, local_sem.at[1])

    def load_own(h, which):
        src, dst = ((k_hbm, k_buf), (v_hbm, v_buf))[which]
        return pltpu.make_async_copy(
            src.at[:, columns(h)], dst.at[h, pl.ds(MEM, SEG)], own_sem.at[which, h]
        )

    barrier = pltpu.get_barrier_semaphore()

    def greet(to_dp, to_seq):
        pl.semaphore_signal(
            barrier, inc=1, device_id={"dp": to_dp, "seq": to_seq},
            device_id_type=pl.DeviceIdType.MESH,
        )

    greet(dp, seq_at(1))
    greet(dp, seq_at(-1))
    greet(zl * 2 + other, seq)

    @pl.loop(1, NZ)
    def _(p):
        greet(((zl + p) % NZ) * 2 + core, seq)

    @pl.loop(1, PLANE)
    def _(p):
        greet(dp, plane_seq((plane + p) % PLANE))

    load_q.start()
    load_g.start()

    @pl.loop(0, H)
    def _(h):
        load_own(h, 0).start()
        load_own(h, 1).start()

    rows_in = table_ref[:, columns(plane)].astype(F32)
    for r in range(ROWS):
        msg_f[ROWS - 1 - r : ROWS - r, :] = rows_in[r : r + 1, :]
    msg_f[ROWS : ROWS + 1, :] = ub_ref[...].astype(F32)
    msg_f[ROWS + 1 : ROWS + 2, :] = vb_ref[...].astype(F32)
    msg_f[ROWS + 2 : MSG, :] = jnp.zeros((MSG - ROWS - 2, HEAD), F32)
    tz[core, zl] = msg_f[...].astype(BF16)

    pl.semaphore_wait(barrier, PARTNERS)

    def table_z(target, sem):
        return remote(tz.at[core, zl], tz.at[core, zl], tz_s.at[target], tz_r.at[sem], target * 2 + core, seq)

    @pl.loop(1, NZ)
    def _(p):
        table_z((zl + p) % NZ, zl).start()

    def halo(h, which, step):
        src, dst = ((k_hbm, k_buf), (v_hbm, v_buf))[which]
        return remote(
            src.at[:, columns(h)], dst.at[h, pl.ds(MEM - step * SEG, SEG)],
            halo_s.at[which, step - 1, h], halo_r.at[which, step - 1, h], dp, seq_at(step),
        )

    @pl.loop(0, H)
    def _(h):
        for step in (1, 2):
            for which in (0, 1):
                halo(h, which, step).start()

    @pl.loop(1, NZ)
    def _(p):
        source = (zl + p) % NZ
        remote(tz.at[core, zl], tz.at[core, source], tz_s.at[source], tz_r.at[source], source * 2 + core, seq).wait_recv()

    sib_table = remote(tz.at[core], tz.at[core], sib_s.at[0], sib_r.at[0], zl * 2 + other, seq)
    sib_table.start()
    remote(tz.at[core], tz.at[other], sib_s.at[0], sib_r.at[0], zl * 2 + other, seq).wait_recv()

    for d in range(DP):
        low = REL - ROWS * (d + 1)
        flat[low : low + ROWS, :] = tz[d % 2, d // 2].astype(F32)[:ROWS]
    table[plane] = flat[...].astype(BF16)

    def table_plane(p, slot, target):
        return remote(table.at[plane], table.at[slot], tab_s.at[p], tab_r.at[slot], dp, plane_seq(target))

    @pl.loop(1, PLANE)
    def _(p):
        table_plane(p, plane, (plane + p) % PLANE).start()

    load_q.wait()
    load_g.wait()

    @pl.loop(1, PLANE)
    def _(p):
        source = (plane + p) % PLANE
        table_plane(p, source, source).wait_recv()

    query_index = lax.broadcasted_iota(jnp.int32, (SEG, REL), 0)
    column_index = lax.broadcasted_iota(jnp.int32, (SEG, REL), 1)
    factor = HEAD ** (-0.5)
    mirror = (
        lax.broadcasted_iota(jnp.int32, (SEG, SEG), 0) + lax.broadcasted_iota(jnp.int32, (SEG, SEG), 1) == SEG - 1
    ).astype(F32).astype(BF16)

    def give_back(h, which, step):
        src, dst = ((back_k, got_k), (back_v, got_v))[which]
        rows = pl.ds(MEM - step * SEG, SEG)
        return remote(
            src.at[h, rows], dst.at[h, rows],
            ret_s.at[which, step - 1, h], ret_r.at[which, step - 1, h], dp, seq_at(-step),
        )

    def send_tgrad(h):
        return remote(tgrad_out.at[h], tgrad_in.at[plane], tg_s.at[h], tg_r.at[plane], dp, plane_seq(h))

    @pl.loop(0, H)
    def _(h):
        for which in (0, 1):
            load_own(h, which).wait()
            for step in (1, 2):
                halo(h, which, step).wait_recv()
        at = columns(h)
        query = q_buf[:, at].astype(F32)
        grad = g_buf[:, at]
        biases = tz[h % 2, h // 2].astype(F32)
        content_query = (query + biases[ROWS : ROWS + 1]).astype(BF16)
        position_query = (query + biases[ROWS + 1 : ROWS + 2]).astype(BF16)
        keys = k_buf[h]
        values = v_buf[h]
        rows = table[h]
        positional = pltpu.roll(dot_nt(position_query, rows), REL - SEG + 1, 1, stride=1, stride_axis=0)
        scores = (dot_nt(content_query, keys) + positional) * factor
        allowed = (column_index <= query_index + MEM) & (column_index >= MEM - seq * SEG)
        scores = jnp.where(allowed, scores, -1e30)
        highest = jnp.max(scores, axis=1, keepdims=True)
        raised = jnp.where(allowed, jnp.exp(scores - highest), 0.0)
        weights = raised * (1.0 / jnp.sum(raised, axis=1, keepdims=True))
        rounded = weights.astype(BF16)
        att_ref[:, at] = dot_nn(rounded, values).astype(BF16)
        grad_probs = dot_nt(grad, values)
        mean = jnp.sum(weights * grad_probs, axis=1, keepdims=True)
        grad_scores = (weights * (grad_probs - mean) * factor).astype(BF16)
        backwards = dot_nn(mirror, grad_scores)
        skewed = dot_nn(mirror, pltpu.roll(backwards, 0, 1, stride=1, stride_axis=0).astype(BF16)).astype(BF16)
        grad_content = dot_nn(grad_scores, keys)
        grad_position = dot_nn(skewed, rows)
        qg_ref[:, at] = (grad_content + grad_position).astype(BF16)
        key_part = dot_tn(grad_scores, content_query)
        own_k[h] = key_part[MEM:]
        back_k[h] = key_part[:MEM].astype(BF16)
        value_part = dot_tn(rounded, grad)
        own_v[h] = value_part[MEM:]
        back_v[h] = value_part[:MEM].astype(BF16)
        for step in (1, 2):
            for which in (0, 1):
                give_back(h, which, step).start()
        tgrad_out[h, :REL] = dot_tn(skewed, position_query).astype(BF16)
        content_sum = jnp.sum(grad_content, axis=0, keepdims=True)
        position_sum = jnp.sum(grad_position, axis=0, keepdims=True)
        content_high = content_sum.astype(BF16).astype(F32)
        position_high = position_sum.astype(BF16).astype(F32)
        line = lax.broadcasted_iota(jnp.int32, (TGRAD - REL, HEAD), 0)
        sums = jnp.where(line == 0, content_high, jnp.where(line == 1, content_sum - content_high, jnp.where(
            line == 2, position_high, jnp.where(line == 3, position_sum - position_high, 0.0))))
        tgrad_out[h, REL:] = sums.astype(BF16)

        @pl.when(h != plane)
        def _():
            send_tgrad(h).start()

    flat[...] = tgrad_out[plane, :REL].astype(F32)
    msg_f[0:16, :] = tgrad_out[plane, REL:].astype(F32)

    @pl.loop(1, PLANE)
    def _(p):
        source = (plane + p) % PLANE
        remote(tgrad_out.at[source], tgrad_in.at[source], tg_s.at[source], tg_r.at[source], dp, plane_seq(source)).wait_recv()
        flat[...] += tgrad_in[source, :REL].astype(F32)
        msg_f[0:16, :] += tgrad_in[source, REL:].astype(F32)

    tail_rows = msg_f[0:16, :]
    content_total = tail_rows[0:1] + tail_rows[1:2]
    position_total = tail_rows[2:3] + tail_rows[3:4]
    line = lax.broadcasted_iota(jnp.int32, (MSG - ROWS, HEAD), 0)
    sums = jnp.where(line == 0, content_total, jnp.where(line == 1, position_total, 0.0))
    for d in range(DP):
        low = REL - ROWS * (d + 1)
        parts[d % 2, d // 2, :ROWS] = flat[low : low + ROWS, :]
        parts[d % 2, d // 2, ROWS:] = sums

    sib_parts = remote(parts.at[other], sib_in, sib_s.at[1], sib_r.at[1], zl * 2 + other, seq)
    sib_parts.start()
    sib_parts.wait_recv()
    parts[core] += sib_in[...]

    def send_half(target, slot):
        return remote(parts.at[core, target], half_in.at[slot], half_s.at[target], half_r.at[slot], target * 2 + core, seq)

    @pl.loop(1, NZ)
    def _(p):
        send_half((zl + p) % NZ, zl).start()

    pair_out[...] = parts[core, zl]

    @pl.loop(1, NZ)
    def _(p):
        source = (zl + p) % NZ
        send_half(source, source).wait_recv()
        pair_out[...] += half_in[source]

    pair = remote(pair_out, pair_in, pair_s, pair_r, dp, plane * 2 + 1 - zh)
    pair.start()
    pair.wait_recv()
    fin[plane] = pair_out[...] + pair_in[...]

    def send_fin(p, slot, target):
        return remote(fin.at[plane], fin.at[slot], fin_s.at[p], fin_r.at[slot], dp, plane_seq(target))

    @pl.loop(1, PLANE)
    def _(p):
        send_fin(p, plane, (plane + p) % PLANE).start()

    @pl.loop(1, PLANE)
    def _(p):
        source = (plane + p) % PLANE
        send_fin(p, source, source).wait_recv()

    @pl.loop(0, H)
    def _(h):
        tg_ref[:, columns(h)] = fin[h, :ROWS]

    mine = fin[dp]
    cg_ref[...] = mine[ROWS : ROWS + 1]
    pg_ref[...] = mine[ROWS + 1 : ROWS + 2]

    @pl.loop(0, H)
    def _(h):
        for which in (0, 1):
            for step in (1, 2):
                give_back(h, which, step).wait_recv()
        at = columns(h)
        kg_ref[:, at] = (own_k[h] + got_k[h, :SEG].astype(F32) + got_k[h, SEG:].astype(F32)).astype(BF16)
        vg_ref[:, at] = (own_v[h] + got_v[h, :SEG].astype(F32) + got_v[h, SEG:].astype(F32)).astype(BF16)

    sib_table.wait_send()
    sib_parts.wait_send()
    pair.wait_send()

    @pl.loop(1, NZ)
    def _(p):
        target = (zl + p) % NZ
        table_z(target, zl).wait_send()
        send_half(target, zl).wait_send()

    @pl.loop(1, PLANE)
    def _(p):
        target = (plane + p) % PLANE
        table_plane(p, plane, target).wait_send()
        send_fin(p, plane, target).wait_send()
        send_tgrad(target).wait_send()

    @pl.loop(0, H)
    def _(h):
        for step in (1, 2):
            for which in (0, 1):
                halo(h, which, step).wait_send()
                give_back(h, which, step).wait_send()


def local(queries, keys, values, position_keys, content_bias, position_bias, out_grad):
    any_space = pl.BlockSpec(memory_space=pl.ANY)
    vmem = pl.BlockSpec(memory_space=pltpu.VMEM)
    block = jax.ShapeDtypeStruct((SEG, HD), BF16)
    line = jax.ShapeDtypeStruct((1, HEAD), F32)
    dma = pltpu.SemaphoreType.DMA
    heads = lambda rows, dtype: pltpu.VMEM((H, rows, HEAD), dtype)
    attended, query_grad, key_grad, value_grad, table_grad, content_grad, position_grad = pl.pallas_call(
        kernel,
        out_shape=(block, block, block, block, jax.ShapeDtypeStruct((ROWS, HD), F32), line, line),
        in_specs=[any_space] * 4 + [vmem] * 3,
        out_specs=(vmem,) * 7,
        scratch_shapes=[
            pltpu.VMEM((SEG, HD), BF16),
            pltpu.VMEM((SEG, HD), BF16),
            heads(REL, BF16),
            heads(REL, BF16),
            heads(SEG, F32),
            heads(SEG, F32),
            heads(MEM, BF16),
            heads(MEM, BF16),
            heads(MEM, BF16),
            heads(MEM, BF16),
            pltpu.VMEM((MSG, HEAD), F32),
            pltpu.VMEM((2, NZ, MSG, HEAD), BF16),
            pltpu.VMEM((REL, HEAD), F32),
            heads(REL, BF16),
            heads(TGRAD, BF16),
            heads(TGRAD, BF16),
            pltpu.VMEM((2, NZ, MSG, HEAD), F32),
            pltpu.VMEM((NZ, MSG, HEAD), F32),
            pltpu.VMEM((NZ, MSG, HEAD), F32),
            pltpu.VMEM((MSG, HEAD), F32),
            pltpu.VMEM((MSG, HEAD), F32),
            heads(MSG, F32),
            dma((2,)),
            dma((2, H)),
            dma((2, 2, H)),
            dma((2, 2, H)),
            dma((2, 2, H)),
            dma((2, 2, H)),
            dma((NZ,)),
            dma((NZ,)),
            dma((2,)),
            dma((2,)),
            dma((PLANE,)),
            dma((PLANE,)),
            dma((H,)),
            dma((PLANE,)),
            dma((NZ,)),
            dma((NZ,)),
            dma,
            dma,
            dma((PLANE,)),
            dma((PLANE,)),
        ],
        compiler_params=pltpu.CompilerParams(
            collective_id=0, has_side_effects=True, vmem_limit_bytes=48 * 2**20
        ),
    )(
        queries[0], keys[0], values[0], out_grad[0],
        position_keys, content_bias[None], position_bias[None],
    )
    return (
        attended[None],
        query_grad[None],
        key_grad[None],
        value_grad[None],
        jnp.flip(table_grad, axis=0),
        content_grad[0],
        position_grad[0],
    )


def solution(mesh):
    placed = (
        P("dp", "seq", None),
        P("dp", "seq", None),
        P("dp", "seq", None),
        P("dp", None),
        P("dp"),
        P("dp"),
        P("dp", "seq", None),
    )
    return jax.shard_map(
        local,
        mesh=mesh,
        in_specs=placed,
        out_specs=(
            P("dp", "seq", None),
            P("dp", "seq", None),
            P("dp", "seq", None),
            P("dp", "seq", None),
            P("dp", None),
            P("dp"),
            P("dp"),
        ),
        check_vma=False,
    )
```

```python
import functools

import jax
import jax.numpy as jnp
from jax import lax
from jax.experimental import pallas as pl
from jax.experimental.pallas import tpu as pltpu
from jax.sharding import PartitionSpec as P

H = 16
HEAD = 128
SEG = 128
MEM = 256
HD = 2048
REL = 384
DP = 16
NZ = 8
PLANE = 16
ROWS = REL // DP
MSG = 32
TGRAD = REL + 16
STAT = 3
STAGES = (1, 6)
RELEASE = (4, 2)
PARTNERS = (PLANE - 1) + 2 * (NZ - 1) + 1 + 2

F32 = jnp.float32
BF16 = jnp.bfloat16


def dot_nt(a, b):
    return lax.dot_general(a, b, (((1,), (1,)), ((), ())), preferred_element_type=F32)


def dot_nn(a, b):
    return lax.dot_general(a, b, (((1,), (0,)), ((), ())), preferred_element_type=F32)


def dot_tn(a, b):
    return lax.dot_general(a, b, (((0,), (0,)), ((), ())), preferred_element_type=F32)


def columns(head):
    return pl.ds(pl.multiple_of(head * HEAD, HEAD), HEAD)


def kernel(
    q_hbm, k_hbm, v_hbm, g_hbm, table_ref, ub_ref, vb_ref,
    att_ref, qg_ref, kg_ref, vg_ref, tg_ref, cg_ref, pg_ref,
    q_buf, g_buf, k_buf, v_buf, own_k, own_v, query_in, grad_in, stats, stats_out, stats_in, stats_rows,
    msg_f, tz, flat, table, tgrad_out, tgrad_in, parts, sib_in, half_out, half_in, fin,
    local_sem, own_sem, halo_s, halo_r, stat_s, stat_r, tz_s, tz_r, sib_s, sib_r,
    tab_s, tab_r, tg_s, tg_r, half_s, half_r, fin_s, fin_r,
):
    dp = lax.axis_index("dp")
    seq = lax.axis_index("seq")
    zl = dp // 2
    core = dp % 2
    other = 1 - core
    plane = seq // 2
    zh = seq % 2

    def remote(src, dst, ss, rs, to_dp, to_seq):
        return pltpu.make_async_remote_copy(
            src_ref=src, dst_ref=dst, send_sem=ss, recv_sem=rs,
            device_id={"dp": to_dp, "seq": to_seq}, device_id_type=pl.DeviceIdType.MESH,
        )

    def seq_at(step):
        return (seq + step + 32) % 32

    def plane_seq(p):
        return p * 2 + zh

    def turn(i, step):
        return (i + seq_at(step) // 2) % H

    load_q = pltpu.make_async_copy(q_hbm, q_buf, local_sem.at[0])
    load_g = pltpu.make_async_copy(g_hbm, g_buf, local_sem.at[1])

    def load_own(h, which):
        src, dst = ((k_hbm, k_buf), (v_hbm, v_buf))[which]
        return pltpu.make_async_copy(
            src.at[:, columns(h)], dst.at[h, pl.ds(MEM, SEG)], own_sem.at[which, h]
        )

    barrier = pltpu.get_barrier_semaphore()

    def greet(to_dp, to_seq):
        pl.semaphore_signal(
            barrier, inc=1, device_id={"dp": to_dp, "seq": to_seq},
            device_id_type=pl.DeviceIdType.MESH,
        )

    greet(dp, seq_at(1))
    greet(dp, seq_at(-1))
    greet(zl * 2 + other, seq)

    @pl.loop(1, NZ)
    def _(p):
        for half in (0, 1):
            greet(((zl + p) % NZ) * 2 + core, plane * 2 + half)

    @pl.loop(1, PLANE)
    def _(p):
        greet(dp, plane_seq((plane + p) % PLANE))

    load_q.start()
    load_g.start()

    @pl.loop(0, H)
    def _(i):
        load_own(turn(i, 0), 0).start()
        load_own(turn(i, 0), 1).start()

    rows_in = table_ref[:, columns(plane)].astype(F32)
    for r in range(ROWS):
        msg_f[ROWS - 1 - r : ROWS - r, :] = rows_in[r : r + 1, :]
    msg_f[ROWS : ROWS + 1, :] = ub_ref[...].astype(F32)
    msg_f[ROWS + 1 : ROWS + 2, :] = vb_ref[...].astype(F32)
    msg_f[ROWS + 2 : MSG, :] = jnp.zeros((MSG - ROWS - 2, HEAD), F32)
    tz[core, zl] = msg_f[...].astype(BF16)

    stats[...] = jnp.zeros_like(stats)

    pl.semaphore_wait(barrier, PARTNERS)

    def table_z(target, sem):
        return remote(tz.at[core, zl], tz.at[core, zl], tz_s.at[target], tz_r.at[sem], target * 2 + core, seq)

    @pl.loop(1, NZ)
    def _(p):
        table_z((zl + p) % NZ, zl).start()

    def halo(h, which, step):
        src = (k_hbm, v_hbm, q_hbm, g_hbm)[which]
        dst = (k_buf, v_buf, query_in, grad_in)[which]
        low, target = (MEM - step * SEG, seq_at(step)) if which < 2 else ((step - 1) * SEG, seq_at(-step))
        return remote(
            src.at[:, columns(h)], dst.at[h, pl.ds(low, SEG)],
            halo_s.at[which, step - 1, h], halo_r.at[which, step - 1, h], dp, target,
        )

    @pl.loop(1, NZ)
    def _(p):
        source = (zl + p) % NZ
        remote(tz.at[core, zl], tz.at[core, source], tz_s.at[source], tz_r.at[source], source * 2 + core, seq).wait_recv()

    sib_table = remote(tz.at[core], tz.at[core], sib_s.at[0], sib_r.at[0], zl * 2 + other, seq)
    sib_table.start()

    @pl.loop(0, H)
    def _(i):
        for which in (0, 1):
            halo(turn(i, 1), which, 1).start()

    remote(tz.at[core], tz.at[other], sib_s.at[0], sib_r.at[0], zl * 2 + other, seq).wait_recv()

    for d in range(DP):
        low = REL - ROWS * (d + 1)
        flat[low : low + ROWS, :] = tz[d % 2, d // 2].astype(F32)[:ROWS]
    table[plane] = flat[...].astype(BF16)

    def table_plane(p, slot, target):
        return remote(table.at[plane], table.at[slot], tab_s.at[p], tab_r.at[slot], dp, plane_seq(target))

    @pl.loop(1, PLANE)
    def _(p):
        table_plane(p, plane, (plane - p + PLANE) % PLANE).start()

    @pl.loop(0, H)
    def _(i):
        for which in (0, 1):
            halo(turn(i, 2), which, 2).start()

    @pl.loop(0, H)
    def _(i):
        for which in (2, 3):
            halo(turn(i, -2), which, 2).start()

    load_q.wait()
    load_g.wait()

    query_index = lax.broadcasted_iota(jnp.int32, (SEG, REL), 0)
    column_index = lax.broadcasted_iota(jnp.int32, (SEG, REL), 1)
    factor = HEAD ** (-0.5)
    mirror = (
        lax.broadcasted_iota(jnp.int32, (SEG, SEG), 0) + lax.broadcasted_iota(jnp.int32, (SEG, SEG), 1) == SEG - 1
    ).astype(F32).astype(BF16)

    lane_index = lax.broadcasted_iota(jnp.int32, (SEG, HEAD), 1)
    half_heads = H // 2

    def with_biases(query, h):
        biases = tz[h % 2, h // 2].astype(F32)
        query = query.astype(F32)
        return (query + biases[ROWS : ROWS + 1]).astype(BF16), (query + biases[ROWS + 1 : ROWS + 2]).astype(BF16)

    def send_stats(group, step):
        rows = pl.ds(group * STAT * half_heads, STAT * half_heads)
        return remote(
            stats_out.at[rows], stats_in.at[step - 1, rows],
            stat_s.at[group, step - 1], stat_r.at[group, step - 1], dp, seq_at(-step),
        )

    def send_tgrad(h):
        return remote(tgrad_out.at[h], tgrad_in.at[plane], tg_s.at[h], tg_r.at[plane], dp, plane_seq(h))

    @pl.loop(0, H)
    def _(i):
        h = turn(i, 0)

        @pl.when(h != plane)
        def _():
            table_plane(0, h, h).wait_recv()

        for which in (0, 1):
            load_own(h, which).wait()
            for step in (1, 2):
                halo(h, which, step).wait_recv()
        at = columns(h)
        grad = g_buf[:, at]
        content_query, position_query = with_biases(q_buf[:, at], h)
        keys = k_buf[h]
        values = v_buf[h]
        rows = table[h]
        positional = pltpu.roll(dot_nt(position_query, rows), REL - SEG + 1, 1, stride=1, stride_axis=0)
        scores = (dot_nt(content_query, keys) + positional) * factor
        allowed = (column_index <= query_index + MEM) & (column_index >= MEM - seq * SEG)
        scores = jnp.where(allowed, scores, -1e30)
        highest = jnp.max(scores, axis=1, keepdims=True)
        raised = jnp.where(allowed, jnp.exp(scores - highest), 0.0)
        inverse = 1.0 / jnp.sum(raised, axis=1, keepdims=True)
        weights = raised * inverse
        rounded = weights.astype(BF16)
        att_ref[:, at] = dot_nn(rounded, values).astype(BF16)
        grad_probs = dot_nt(grad, values)
        mean = jnp.sum(weights * grad_probs, axis=1, keepdims=True)
        grad_scores = (weights * (grad_probs - mean) * factor).astype(BF16)
        backwards = dot_nn(mirror, grad_scores)
        skewed = dot_nn(mirror, pltpu.roll(backwards, 0, 1, stride=1, stride_axis=0).astype(BF16)).astype(BF16)
        grad_content = dot_nn(grad_scores, keys)
        grad_position = dot_nn(skewed, rows)
        qg_ref[:, at] = (grad_content + grad_position).astype(BF16)
        own_k[h] = dot_tn(grad_scores[:, MEM:], content_query)
        own_v[h] = dot_tn(rounded[:, MEM:], grad)
        base = i * STAT
        stats[...] = jnp.where(lane_index == base, highest, jnp.where(
            lane_index == base + 1, inverse, jnp.where(lane_index == base + 2, mean, stats[...])))

        for group in (0, 1):
            @pl.when(i == half_heads * (group + 1) - 1)
            def _():
                flipped = stats[...].T
                rows = slice(group * STAT * half_heads, (group + 1) * STAT * half_heads)
                stats_out[rows] = flipped[rows]
                for step in (1, 2):
                    send_stats(group, step).start()

        first, each = RELEASE
        @pl.when((i >= first) & (i < first + H // each))
        def _():
            for j in range(each):
                for which in (2, 3):
                    halo(turn((i - first) * each + j, -1), which, 1).start()

        tgrad_out[h, :REL] = dot_tn(skewed, position_query).astype(BF16)
        content_sum = jnp.sum(grad_content, axis=0, keepdims=True)
        position_sum = jnp.sum(grad_position, axis=0, keepdims=True)
        content_high = content_sum.astype(BF16).astype(F32)
        position_high = position_sum.astype(BF16).astype(F32)
        line = lax.broadcasted_iota(jnp.int32, (TGRAD - REL, HEAD), 0)
        sums = jnp.where(line == 0, content_high, jnp.where(line == 1, content_sum - content_high, jnp.where(
            line == 2, position_high, jnp.where(line == 3, position_sum - position_high, 0.0))))
        tgrad_out[h, REL:] = sums.astype(BF16)

        @pl.when(h != plane)
        def _():
            send_tgrad(h).start()

    flat[...] = tgrad_out[plane, :REL].astype(F32)
    msg_f[0:16, :] = tgrad_out[plane, REL:].astype(F32)

    @pl.loop(1, PLANE)
    def _(p):
        source = (plane + p) % PLANE
        remote(tgrad_out.at[source], tgrad_in.at[source], tg_s.at[source], tg_r.at[source], dp, plane_seq(source)).wait_recv()
        flat[...] += tgrad_in[source, :REL].astype(F32)
        msg_f[0:16, :] += tgrad_in[source, REL:].astype(F32)

    tail_rows = msg_f[0:16, :]
    content_total = tail_rows[0:1] + tail_rows[1:2]
    position_total = tail_rows[2:3] + tail_rows[3:4]
    line = lax.broadcasted_iota(jnp.int32, (MSG - ROWS, HEAD), 0)
    sums = jnp.where(line == 0, content_total, jnp.where(line == 1, position_total, 0.0))
    for d in range(DP):
        low = REL - ROWS * (d + 1)
        parts[d % 2, d // 2, :ROWS] = flat[low : low + ROWS, :]
        parts[d % 2, d // 2, ROWS:] = sums

    sib_parts = remote(parts.at[other], sib_in, sib_s.at[1], sib_r.at[1], zl * 2 + other, seq)
    sib_parts.start()

    def send_half(half, target, slot):
        return remote(
            half_out.at[target], half_in.at[slot], half_s.at[half, target], half_r.at[slot],
            target * 2 + core, plane * 2 + half,
        )

    def along_z(act):
        act(1 - zh, zl)

        @pl.loop(1, NZ)
        def _(p):
            act(zh, (zl + p) % NZ)
            act(1 - zh, (zl + p) % NZ)

    def send_fin(p, slot, target):
        return remote(fin.at[plane], fin.at[slot], fin_s.at[p], fin_r.at[slot], dp, plane_seq(target))

    def take_stats(i, step):
        for group in (0, 1):
            @pl.when(i == half_heads * group)
            def _():
                send_stats(group, step).wait_recv()
                lanes = slice(group * STAT * half_heads, (group + 1) * STAT * half_heads)
                padded = jnp.concatenate([stats_in[step - 1, lanes]] * 2 + [
                    jnp.zeros((SEG - 2 * STAT * half_heads, HEAD), F32)], axis=0)
                stats_rows[step - 1] = padded.T

    def later_part(h, step):
        content_query, position_query = with_biases(query_in[h, (step - 1) * SEG : step * SEG], h)
        grad = grad_in[h, (step - 1) * SEG : step * SEG]
        rows = table[h, MEM - step * SEG : 2 * MEM - step * SEG]
        positional = pltpu.roll(dot_nt(position_query, rows), SEG + 1, 1, stride=1, stride_axis=0)[:, :SEG]
        scores = (dot_nt(content_query, k_buf[h, MEM:]) + positional) * factor
        base = ((h - seq_at(step) // 2 + H) % H) * STAT
        column = lambda at: jnp.sum(
            jnp.where(lane_index == base + at, stats_rows[step - 1], 0.0), axis=1, keepdims=True)
        weights = jnp.where(
            lane_index < (32 - step - seq) * HEAD, jnp.exp(scores - column(0)) * column(1), 0.0)
        grad_probs = dot_nt(grad, v_buf[h, MEM:])
        grad_scores = (weights * (grad_probs - column(2)) * factor).astype(BF16)
        return dot_tn(grad_scores, content_query), dot_tn(weights.astype(BF16), grad)

    @pl.loop(0, H)
    def _(i):
        @pl.when(i == STAGES[0])
        def _():
            sib_parts.wait_recv()
            parts[core] += sib_in[...]
            low = lax.broadcasted_iota(jnp.int32, (MSG, HEAD), 0)

            @pl.loop(0, NZ)
            def _(p):
                block = parts[core, p]
                rest = block - block.astype(BF16).astype(F32)
                block = jnp.where(low == ROWS + 2, rest[ROWS : ROWS + 1], jnp.where(
                    low == ROWS + 3, rest[ROWS + 1 : ROWS + 2], block))
                half_out[p] = block.astype(BF16)

            along_z(lambda half, target: send_half(half, target, zh * NZ + zl).start())

        h = turn(i, 2)
        take_stats(i, 2)
        for which in (2, 3):
            halo(h, which, 2).wait_recv()
        key_part, value_part = later_part(h, 2)
        own_k[h] += key_part
        own_v[h] += value_part

    @pl.loop(0, H)
    def _(i):
        @pl.when(i == STAGES[1])
        def _():
            fin[plane] = half_out[zl].astype(F32)

            def add(half, source):
                slot = half * NZ + source
                remote(half_out.at[source], half_in.at[slot], half_s.at[half, source], half_r.at[slot],
                       source * 2 + core, plane * 2 + half).wait_recv()
                fin[plane] += half_in[slot].astype(F32)

            along_z(add)
            total = fin[plane]
            for r in range(ROWS):
                fin[plane, r : r + 1] = total[ROWS - 1 - r : ROWS - r]

            @pl.loop(1, PLANE)
            def _(p):
                send_fin(p, plane, (plane + p) % PLANE).start()

        h = turn(i, 1)
        take_stats(i, 1)
        for which in (2, 3):
            halo(h, which, 1).wait_recv()
        key_part, value_part = later_part(h, 1)
        at = columns(h)
        kg_ref[:, at] = (own_k[h] + key_part).astype(BF16)
        vg_ref[:, at] = (own_v[h] + value_part).astype(BF16)

    @pl.loop(1, PLANE)
    def _(p):
        source = (plane + p) % PLANE
        send_fin(p, source, source).wait_recv()

    @pl.loop(0, H)
    def _(h):
        tg_ref[:, columns(h)] = fin[h, :ROWS]

    mine = fin[dp]
    cg_ref[...] = mine[ROWS : ROWS + 1] + mine[ROWS + 2 : ROWS + 3]
    pg_ref[...] = mine[ROWS + 1 : ROWS + 2] + mine[ROWS + 3 : ROWS + 4]

    sib_table.wait_send()
    sib_parts.wait_send()

    @pl.loop(1, NZ)
    def _(p):
        target = (zl + p) % NZ
        table_z(target, zl).wait_send()

    @pl.loop(1, PLANE)
    def _(p):
        target = (plane + p) % PLANE
        table_plane(p, plane, (plane - p + PLANE) % PLANE).wait_send()
        send_fin(p, plane, target).wait_send()
        send_tgrad(target).wait_send()

    along_z(lambda half, target: send_half(half, target, zh * NZ + zl).wait_send())
    for step in (1, 2):
        for group in (0, 1):
            send_stats(group, step).wait_send()

    @pl.loop(0, H)
    def _(h):
        for step in (1, 2):
            for which in range(4):
                halo(h, which, step).wait_send()


def local(queries, keys, values, position_keys, content_bias, position_bias, out_grad):
    hbm = pl.BlockSpec(memory_space=pltpu.HBM)
    vmem = pl.BlockSpec(memory_space=pltpu.VMEM)
    block = jax.ShapeDtypeStruct((SEG, HD), BF16)
    line = jax.ShapeDtypeStruct((1, HEAD), F32)
    dma = pltpu.SemaphoreType.DMA
    heads = lambda rows, dtype: pltpu.VMEM((H, rows, HEAD), dtype)
    attended, query_grad, key_grad, value_grad, table_grad, content_grad, position_grad = pl.pallas_call(
        kernel,
        out_shape=(block, block, block, block, jax.ShapeDtypeStruct((ROWS, HD), F32), line, line),
        in_specs=[hbm] * 4 + [vmem] * 3,
        out_specs=(vmem,) * 7,
        scratch_shapes=[
            pltpu.VMEM((SEG, HD), BF16),
            pltpu.VMEM((SEG, HD), BF16),
            heads(REL, BF16),
            heads(REL, BF16),
            heads(SEG, F32),
            heads(SEG, F32),
            heads(MEM, BF16),
            heads(MEM, BF16),
            pltpu.VMEM((SEG, HEAD), F32),
            pltpu.VMEM((STAT * H, HEAD), F32),
            pltpu.VMEM((2, STAT * H, HEAD), F32),
            pltpu.VMEM((2, SEG, HEAD), F32),
            pltpu.VMEM((MSG, HEAD), F32),
            pltpu.VMEM((2, NZ, MSG, HEAD), BF16),
            pltpu.VMEM((REL, HEAD), F32),
            heads(REL, BF16),
            heads(TGRAD, BF16),
            heads(TGRAD, BF16),
            pltpu.VMEM((2, NZ, MSG, HEAD), F32),
            pltpu.VMEM((NZ, MSG, HEAD), F32),
            pltpu.VMEM((NZ, MSG, HEAD), BF16),
            pltpu.VMEM((2 * NZ, MSG, HEAD), BF16),
            heads(MSG, F32),
            dma((2,)),
            dma((2, H)),
            dma((4, 2, H)),
            dma((4, 2, H)),
            dma((2, 2)),
            dma((2, 2)),
            dma((NZ,)),
            dma((NZ,)),
            dma((2,)),
            dma((2,)),
            dma((PLANE,)),
            dma((PLANE,)),
            dma((H,)),
            dma((PLANE,)),
            dma((2, NZ)),
            dma((2 * NZ,)),
            dma((PLANE,)),
            dma((PLANE,)),
        ],
        compiler_params=pltpu.CompilerParams(
            collective_id=0, has_side_effects=True, vmem_limit_bytes=60 * 2**20
        ),
    )(
        queries[0], keys[0], values[0], out_grad[0],
        position_keys, content_bias[None], position_bias[None],
    )
    return (
        attended[None],
        query_grad[None],
        key_grad[None],
        value_grad[None],
        table_grad,
        content_grad[0],
        position_grad[0],
    )


def solution(mesh):
    placed = (
        P("dp", "seq", None),
        P("dp", "seq", None),
        P("dp", "seq", None),
        P("dp", None),
        P("dp"),
        P("dp"),
        P("dp", "seq", None),
    )
    return jax.shard_map(
        local,
        mesh=mesh,
        in_specs=placed,
        out_specs=(
            P("dp", "seq", None),
            P("dp", "seq", None),
            P("dp", "seq", None),
            P("dp", "seq", None),
            P("dp", None),
            P("dp"),
            P("dp"),
        ),
        check_vma=False,
    )
```

```python
import functools

import jax
import jax.numpy as jnp
from jax import lax
from jax.experimental import pallas as pl
from jax.experimental.pallas import tpu as pltpu
from jax.sharding import PartitionSpec as P

H = 16
HEAD = 128
SEG = 128
MEM = 256
HD = 2048
REL = 384
DP = 16
NZ = 8
PLANE = 16
ROWS = REL // DP
MSG = 32
TGRAD = REL + 16
STAT = 3
STAGES = (1, 2, 15)
WINDOW = 10
SPAN = 8
PARTNERS = (PLANE - 1) + 2 * (NZ - 1) + 1 + 2

F32 = jnp.float32
BF16 = jnp.bfloat16


def dot_nt(a, b):
    return lax.dot_general(a, b, (((1,), (1,)), ((), ())), preferred_element_type=F32)


def dot_nn(a, b):
    return lax.dot_general(a, b, (((1,), (0,)), ((), ())), preferred_element_type=F32)


def dot_tn(a, b):
    return lax.dot_general(a, b, (((0,), (0,)), ((), ())), preferred_element_type=F32)


def columns(head):
    return pl.ds(pl.multiple_of(head * HEAD, HEAD), HEAD)


def kernel(
    q_hbm, k_hbm, v_hbm, g_hbm, table_ref, ub_ref, vb_ref,
    att_ref, qg_ref, kg_ref, vg_ref, tg_ref, cg_ref, pg_ref,
    q_buf, g_buf, k_buf, v_buf, own_k, own_v, query_in, grad_in, stats, stats_out, stats_in, stats_rows,
    msg_f, tz, flat, table, tgrad_out, tgrad_in, parts, sib_in, half_out, half_in, fin,
    local_sem, own_sem, halo_s, halo_r, stat_s, stat_r, tz_s, tz_r, sib_s, sib_r,
    tab_s, tab_r, tg_s, tg_r, half_s, half_r, fin_s, fin_r,
):
    dp = lax.axis_index("dp")
    seq = lax.axis_index("seq")
    zl = dp // 2
    core = dp % 2
    other = 1 - core
    plane = seq // 2
    zh = seq % 2

    def remote(src, dst, ss, rs, to_dp, to_seq):
        return pltpu.make_async_remote_copy(
            src_ref=src, dst_ref=dst, send_sem=ss, recv_sem=rs,
            device_id={"dp": to_dp, "seq": to_seq}, device_id_type=pl.DeviceIdType.MESH,
        )

    def seq_at(step):
        return (seq + step + 32) % 32

    def plane_seq(p):
        return p * 2 + zh

    def turn(i, step):
        return (i + seq_at(step) // 2) % H

    load_q = pltpu.make_async_copy(q_hbm, q_buf, local_sem.at[0])
    load_g = pltpu.make_async_copy(g_hbm, g_buf, local_sem.at[1])

    def load_own(which):
        src, dst = ((k_hbm, k_buf), (v_hbm, v_buf))[which]
        return pltpu.make_async_copy(src, dst.at[pl.ds(MEM, SEG)], own_sem.at[which])

    barrier = pltpu.get_barrier_semaphore()

    def greet(to_dp, to_seq):
        pl.semaphore_signal(
            barrier, inc=1, device_id={"dp": to_dp, "seq": to_seq},
            device_id_type=pl.DeviceIdType.MESH,
        )

    greet(dp, seq_at(1))
    greet(dp, seq_at(-1))
    greet(zl * 2 + other, seq)

    @pl.loop(1, NZ)
    def _(p):
        for half in (0, 1):
            greet(((zl + p) % NZ) * 2 + core, plane * 2 + half)

    @pl.loop(1, PLANE)
    def _(p):
        greet(dp, plane_seq((plane + p) % PLANE))

    load_q.start()
    load_g.start()

    load_own(0).start()
    load_own(1).start()

    rows_in = table_ref[:, columns(plane)].astype(F32)
    for r in range(ROWS):
        msg_f[ROWS - 1 - r : ROWS - r, :] = rows_in[r : r + 1, :]
    msg_f[ROWS : ROWS + 1, :] = ub_ref[...].astype(F32)
    msg_f[ROWS + 1 : ROWS + 2, :] = vb_ref[...].astype(F32)
    msg_f[ROWS + 2 : MSG, :] = jnp.zeros((MSG - ROWS - 2, HEAD), F32)
    tz[core, zl] = msg_f[...].astype(BF16)

    stats[...] = jnp.zeros_like(stats)

    pl.semaphore_wait(barrier, PARTNERS)

    def table_z(target, sem):
        return remote(tz.at[core, zl], tz.at[core, zl], tz_s.at[target], tz_r.at[sem], target * 2 + core, seq)

    @pl.loop(1, NZ)
    def _(p):
        table_z((zl + p) % NZ, zl).start()

    def halo(h, which, step):
        src = (k_hbm, v_hbm, q_hbm, g_hbm)[which]
        dst = (k_buf, v_buf, query_in, grad_in)[which]
        low, target = (MEM - step * SEG, seq_at(step)) if which < 2 else ((step - 1) * SEG, seq_at(-step))
        return remote(
            src.at[:, columns(h)], dst.at[pl.ds(low, SEG), columns(h)],
            halo_s.at[which, step - 1, h], halo_r.at[which, step - 1, h], dp, target,
        )

    @pl.loop(1, NZ)
    def _(p):
        source = (zl + p) % NZ
        remote(tz.at[core, zl], tz.at[core, source], tz_s.at[source], tz_r.at[source], source * 2 + core, seq).wait_recv()

    sib_table = remote(tz.at[core], tz.at[core], sib_s.at[0], sib_r.at[0], zl * 2 + other, seq)
    sib_table.start()

    def beside(group, which):
        src = (k_hbm, v_hbm, q_hbm, g_hbm)[which]
        dst = (k_buf, v_buf, query_in, grad_in)[which]
        low, target = (0, seq_at(2)) if which < 2 else (SEG, seq_at(-2))
        at = pl.ds(pl.multiple_of(group * SPAN * HEAD, HEAD), SPAN * HEAD)
        return remote(
            src.at[:, at], dst.at[pl.ds(low, SEG), at],
            halo_s.at[which, 1, group], halo_r.at[which, 1, group], dp, target,
        )

    def feed(n):
        @pl.when(n < H)
        def _():
            for which in (0, 1):
                halo(turn(n, 1), which, 1).start()

        @pl.when((n >= H) & (n < 2 * H))
        def _():
            for which in (2, 3):
                halo(turn(n - H, -1), which, 1).start()

    @pl.loop(0, WINDOW)
    def _(n):
        feed(n)

    remote(tz.at[core], tz.at[other], sib_s.at[0], sib_r.at[0], zl * 2 + other, seq).wait_recv()

    for d in range(DP):
        low = REL - ROWS * (d + 1)
        flat[low : low + ROWS, :] = tz[d % 2, d // 2].astype(F32)[:ROWS]
    table[plane] = flat[...].astype(BF16)

    def table_plane(p, slot, target):
        return remote(table.at[plane], table.at[slot], tab_s.at[p], tab_r.at[slot], dp, plane_seq(target))

    @pl.loop(1, PLANE)
    def _(p):
        table_plane(p, plane, (plane - p + PLANE) % PLANE).start()

    @pl.loop(0, H // SPAN)
    def _(i):
        for which in (0, 1):
            beside((turn(0, 2) // SPAN + i) % (H // SPAN), which).start()

    @pl.loop(0, H // SPAN)
    def _(i):
        for which in (2, 3):
            beside((turn(0, -2) // SPAN + i) % (H // SPAN), which).start()

    load_q.wait()
    load_g.wait()

    query_index = lax.broadcasted_iota(jnp.int32, (SEG, REL), 0)
    column_index = lax.broadcasted_iota(jnp.int32, (SEG, REL), 1)
    factor = HEAD ** (-0.5)
    mirror = (
        lax.broadcasted_iota(jnp.int32, (SEG, SEG), 0) + lax.broadcasted_iota(jnp.int32, (SEG, SEG), 1) == SEG - 1
    ).astype(F32).astype(BF16)

    lane_index = lax.broadcasted_iota(jnp.int32, (SEG, HEAD), 1)
    half_heads = H // 2

    def with_biases(query, h):
        biases = tz[h % 2, h // 2].astype(F32)
        query = query.astype(F32)
        return (query + biases[ROWS : ROWS + 1]).astype(BF16), (query + biases[ROWS + 1 : ROWS + 2]).astype(BF16)

    def send_stats(group, step):
        rows = pl.ds(group * STAT * half_heads, STAT * half_heads)
        return remote(
            stats_out.at[rows], stats_in.at[step - 1, rows],
            stat_s.at[group, step - 1], stat_r.at[group, step - 1], dp, seq_at(-step),
        )

    def send_tgrad(h):
        return remote(tgrad_out.at[h], tgrad_in.at[plane], tg_s.at[h], tg_r.at[plane], dp, plane_seq(h))

    @pl.loop(0, H)
    def _(i):
        h = turn(i, 0)

        @pl.when(h != plane)
        def _():
            table_plane(0, h, h).wait_recv()

        @pl.when(i == 0)
        def _():
            load_own(0).wait()
            load_own(1).wait()

        group = h // SPAN

        @pl.when((i == 0) | ((h % SPAN == 0) & (group != plane // SPAN)))
        def _():
            for which in (0, 1):
                beside(group, which).wait_recv()

        for which in (0, 1):
            halo(h, which, 1).wait_recv()
        feed(i + WINDOW)
        at = columns(h)
        grad = g_buf[:, at]
        content_query, position_query = with_biases(q_buf[:, at], h)
        keys = k_buf[:, at]
        values = v_buf[:, at]
        rows = table[h]
        positional = pltpu.roll(dot_nt(position_query, rows), REL - SEG + 1, 1, stride=1, stride_axis=0)
        scores = (dot_nt(content_query, keys) + positional) * factor
        allowed = (column_index <= query_index + MEM) & (column_index >= MEM - seq * SEG)
        scores = jnp.where(allowed, scores, -1e30)
        highest = jnp.max(scores, axis=1, keepdims=True)
        raised = jnp.where(allowed, jnp.exp(scores - highest), 0.0)
        inverse = 1.0 / jnp.sum(raised, axis=1, keepdims=True)
        weights = raised * inverse
        rounded = weights.astype(BF16)
        att_ref[:, at] = dot_nn(rounded, values).astype(BF16)
        grad_probs = dot_nt(grad, values)
        mean = jnp.sum(weights * grad_probs, axis=1, keepdims=True)
        grad_scores = (weights * (grad_probs - mean) * factor).astype(BF16)
        backwards = dot_nn(mirror, grad_scores)
        skewed = dot_nn(mirror, pltpu.roll(backwards, 0, 1, stride=1, stride_axis=0).astype(BF16)).astype(BF16)
        grad_content = dot_nn(grad_scores, keys)
        grad_position = dot_nn(skewed, rows)
        qg_ref[:, at] = (grad_content + grad_position).astype(BF16)
        own_k[h] = dot_tn(grad_scores[:, MEM:], content_query)
        own_v[h] = dot_tn(rounded[:, MEM:], grad)
        base = i * STAT
        stats[...] = jnp.where(lane_index == base, highest, jnp.where(
            lane_index == base + 1, inverse, jnp.where(lane_index == base + 2, mean, stats[...])))

        for group in (0, 1):
            @pl.when(i == half_heads * (group + 1) - 1)
            def _():
                flipped = stats[...].T
                rows = slice(group * STAT * half_heads, (group + 1) * STAT * half_heads)
                stats_out[rows] = flipped[rows]
                for step in (1, 2):
                    send_stats(group, step).start()

        tgrad_out[h, :REL] = dot_tn(skewed, position_query).astype(BF16)
        content_sum = jnp.sum(grad_content, axis=0, keepdims=True)
        position_sum = jnp.sum(grad_position, axis=0, keepdims=True)
        content_high = content_sum.astype(BF16).astype(F32)
        position_high = position_sum.astype(BF16).astype(F32)
        line = lax.broadcasted_iota(jnp.int32, (TGRAD - REL, HEAD), 0)
        sums = jnp.where(line == 0, content_high, jnp.where(line == 1, content_sum - content_high, jnp.where(
            line == 2, position_high, jnp.where(line == 3, position_sum - position_high, 0.0))))
        tgrad_out[h, REL:] = sums.astype(BF16)

        @pl.when(h != plane)
        def _():
            send_tgrad(h).start()

    sib_parts = remote(parts.at[other], sib_in, sib_s.at[1], sib_r.at[1], zl * 2 + other, seq)

    def send_half(half, target, slot):
        return remote(
            half_out.at[target], half_in.at[slot], half_s.at[half, target], half_r.at[slot],
            target * 2 + core, plane * 2 + half,
        )

    def along_z(act):
        act(1 - zh, zl)

        @pl.loop(1, NZ)
        def _(p):
            act(zh, (zl + p) % NZ)
            act(1 - zh, (zl + p) % NZ)

    def send_fin(p, slot, target):
        return remote(fin.at[plane], fin.at[slot], fin_s.at[p], fin_r.at[slot], dp, plane_seq(target))

    def take_stats(step, groups):
        for group in groups:
            send_stats(group, step).wait_recv()
        width = STAT * half_heads
        taken = [stats_in[step - 1, group * width : (group + 1) * width] for group in groups] * (3 - len(groups))
        taken.append(jnp.zeros((SEG - 2 * width, HEAD), F32))
        stats_rows[step - 1] = jnp.concatenate(taken, axis=0).T

    def later_part(h, step):
        content_query, position_query = with_biases(query_in[(step - 1) * SEG : step * SEG, columns(h)], h)
        grad = grad_in[(step - 1) * SEG : step * SEG, columns(h)]
        rows = table[h, MEM - step * SEG : 2 * MEM - step * SEG]
        positional = pltpu.roll(dot_nt(position_query, rows), SEG + 1, 1, stride=1, stride_axis=0)[:, :SEG]
        scores = (dot_nt(content_query, k_buf[MEM:, columns(h)]) + positional) * factor
        base = ((h - seq_at(step) // 2 + H) % H) * STAT
        column = lambda at: jnp.sum(
            jnp.where(lane_index == base + at, stats_rows[step - 1], 0.0), axis=1, keepdims=True)
        weights = jnp.where(
            lane_index < (32 - step - seq) * HEAD, jnp.exp(scores - column(0)) * column(1), 0.0)
        grad_probs = dot_nt(grad, v_buf[MEM:, columns(h)])
        grad_scores = (weights * (grad_probs - column(2)) * factor).astype(BF16)
        return dot_tn(grad_scores, content_query), dot_tn(weights.astype(BF16), grad)

    @pl.loop(0, H)
    def _(i):
        @pl.when(i == STAGES[0])
        def _():
            flat[...] = tgrad_out[plane, :REL].astype(F32)
            msg_f[0:16, :] = tgrad_out[plane, REL:].astype(F32)

            @pl.loop(1, PLANE)
            def _(p):
                source = (plane + p) % PLANE
                remote(tgrad_out.at[source], tgrad_in.at[source], tg_s.at[source], tg_r.at[source], dp, plane_seq(source)).wait_recv()
                flat[...] += tgrad_in[source, :REL].astype(F32)
                msg_f[0:16, :] += tgrad_in[source, REL:].astype(F32)

            tail_rows = msg_f[0:16, :]
            content_total = tail_rows[0:1] + tail_rows[1:2]
            position_total = tail_rows[2:3] + tail_rows[3:4]
            line = lax.broadcasted_iota(jnp.int32, (MSG - ROWS, HEAD), 0)
            sums = jnp.where(line == 0, content_total, jnp.where(line == 1, position_total, 0.0))
            for d in range(DP):
                low = REL - ROWS * (d + 1)
                parts[d % 2, d // 2, :ROWS] = flat[low : low + ROWS, :]
                parts[d % 2, d // 2, ROWS:] = sums
            sib_parts.start()

        @pl.when(i == STAGES[1])
        def _():
            sib_parts.wait_recv()
            parts[core] += sib_in[...]
            low = lax.broadcasted_iota(jnp.int32, (MSG, HEAD), 0)

            @pl.loop(0, NZ)
            def _(p):
                block = parts[core, p]
                rest = block - block.astype(BF16).astype(F32)
                block = jnp.where(low == ROWS + 2, rest[ROWS : ROWS + 1], jnp.where(
                    low == ROWS + 3, rest[ROWS + 1 : ROWS + 2], block))
                half_out[p] = block.astype(BF16)

            along_z(lambda half, target: send_half(half, target, zh * NZ + zl).start())

        @pl.when(i == STAGES[2])
        def _():
            fin[plane] = half_out[zl].astype(F32)

            def add(half, source):
                slot = half * NZ + source
                remote(half_out.at[source], half_in.at[slot], half_s.at[half, source], half_r.at[slot],
                       source * 2 + core, plane * 2 + half).wait_recv()
                fin[plane] += half_in[slot].astype(F32)

            along_z(add)
            total = fin[plane]
            for r in range(ROWS):
                fin[plane, r : r + 1] = total[ROWS - 1 - r : ROWS - r]

            @pl.loop(1, PLANE)
            def _(p):
                send_fin(p, plane, (plane + p) % PLANE).start()

        h = turn(i, 1)
        @pl.when(i == 0)
        def _():
            take_stats(1, (0,))
            take_stats(2, (0, 1))

            @pl.loop(0, H // SPAN)
            def _(group):
                for which in (2, 3):
                    beside(group, which).wait_recv()

        @pl.when(i == half_heads)
        def _():
            take_stats(1, (1,))

        for which in (2, 3):
            halo(h, which, 1).wait_recv()
        feed(i + H + WINDOW)
        key_near, value_near = later_part(h, 1)
        key_far, value_far = later_part(h, 2)
        at = columns(h)
        kg_ref[:, at] = (own_k[h] + key_near + key_far).astype(BF16)
        vg_ref[:, at] = (own_v[h] + value_near + value_far).astype(BF16)

    @pl.loop(1, PLANE)
    def _(p):
        source = (plane + p) % PLANE
        send_fin(p, source, source).wait_recv()

    @pl.loop(0, H)
    def _(h):
        tg_ref[:, columns(h)] = fin[h, :ROWS]

    mine = fin[dp]
    cg_ref[...] = mine[ROWS : ROWS + 1] + mine[ROWS + 2 : ROWS + 3]
    pg_ref[...] = mine[ROWS + 1 : ROWS + 2] + mine[ROWS + 3 : ROWS + 4]

    sib_table.wait_send()
    sib_parts.wait_send()

    @pl.loop(1, NZ)
    def _(p):
        target = (zl + p) % NZ
        table_z(target, zl).wait_send()

    @pl.loop(1, PLANE)
    def _(p):
        target = (plane + p) % PLANE
        table_plane(p, plane, (plane - p + PLANE) % PLANE).wait_send()
        send_fin(p, plane, target).wait_send()
        send_tgrad(target).wait_send()

    along_z(lambda half, target: send_half(half, target, zh * NZ + zl).wait_send())
    for step in (1, 2):
        for group in (0, 1):
            send_stats(group, step).wait_send()

    @pl.loop(0, H)
    def _(h):
        for which in range(4):
            halo(h, which, 1).wait_send()

    @pl.loop(0, H // SPAN)
    def _(group):
        for which in range(4):
            beside(group, which).wait_send()


def local(queries, keys, values, position_keys, content_bias, position_bias, out_grad):
    hbm = pl.BlockSpec(memory_space=pltpu.HBM)
    vmem = pl.BlockSpec(memory_space=pltpu.VMEM)
    block = jax.ShapeDtypeStruct((SEG, HD), BF16)
    line = jax.ShapeDtypeStruct((1, HEAD), F32)
    dma = pltpu.SemaphoreType.DMA
    heads = lambda rows, dtype: pltpu.VMEM((H, rows, HEAD), dtype)
    attended, query_grad, key_grad, value_grad, table_grad, content_grad, position_grad = pl.pallas_call(
        kernel,
        out_shape=(block, block, block, block, jax.ShapeDtypeStruct((ROWS, HD), F32), line, line),
        in_specs=[hbm] * 4 + [vmem] * 3,
        out_specs=(vmem,) * 7,
        scratch_shapes=[
            pltpu.VMEM((SEG, HD), BF16),
            pltpu.VMEM((SEG, HD), BF16),
            pltpu.VMEM((REL, HD), BF16),
            pltpu.VMEM((REL, HD), BF16),
            heads(SEG, F32),
            heads(SEG, F32),
            pltpu.VMEM((MEM, HD), BF16),
            pltpu.VMEM((MEM, HD), BF16),
            pltpu.VMEM((SEG, HEAD), F32),
            pltpu.VMEM((STAT * H, HEAD), F32),
            pltpu.VMEM((2, STAT * H, HEAD), F32),
            pltpu.VMEM((2, SEG, HEAD), F32),
            pltpu.VMEM((MSG, HEAD), F32),
            pltpu.VMEM((2, NZ, MSG, HEAD), BF16),
            pltpu.VMEM((REL, HEAD), F32),
            heads(REL, BF16),
            heads(TGRAD, BF16),
            heads(TGRAD, BF16),
            pltpu.VMEM((2, NZ, MSG, HEAD), F32),
            pltpu.VMEM((NZ, MSG, HEAD), F32),
            pltpu.VMEM((NZ, MSG, HEAD), BF16),
            pltpu.VMEM((2 * NZ, MSG, HEAD), BF16),
            heads(MSG, F32),
            dma((2,)),
            dma((2,)),
            dma((4, 2, H)),
            dma((4, 2, H)),
            dma((2, 2)),
            dma((2, 2)),
            dma((NZ,)),
            dma((NZ,)),
            dma((2,)),
            dma((2,)),
            dma((PLANE,)),
            dma((PLANE,)),
            dma((H,)),
            dma((PLANE,)),
            dma((2, NZ)),
            dma((2 * NZ,)),
            dma((PLANE,)),
            dma((PLANE,)),
        ],
        compiler_params=pltpu.CompilerParams(
            collective_id=0, has_side_effects=True, vmem_limit_bytes=52 * 2**20
        ),
    )(
        queries[0], keys[0], values[0], out_grad[0],
        position_keys, content_bias[None], position_bias[None],
    )
    return (
        attended[None],
        query_grad[None],
        key_grad[None],
        value_grad[None],
        table_grad,
        content_grad[0],
        position_grad[0],
    )


def solution(mesh):
    placed = (
        P("dp", "seq", None),
        P("dp", "seq", None),
        P("dp", "seq", None),
        P("dp", None),
        P("dp"),
        P("dp"),
        P("dp", "seq", None),
    )
    return jax.shard_map(
        local,
        mesh=mesh,
        in_specs=placed,
        out_specs=(
            P("dp", "seq", None),
            P("dp", "seq", None),
            P("dp", "seq", None),
            P("dp", "seq", None),
            P("dp", None),
            P("dp"),
            P("dp"),
        ),
        check_vma=False,
    )
```

```python
import functools

import jax
import jax.numpy as jnp
from jax import lax
from jax.experimental import pallas as pl
from jax.experimental.pallas import tpu as pltpu
from jax.sharding import PartitionSpec as P

H = 16
HEAD = 128
SEG = 128
MEM = 256
HD = 2048
REL = 384
DP = 16
NZ = 8
PLANE = 16
ROWS = REL // DP
MSG = 32
TGRAD = REL + 16
STAT = 3
STAGES = (1, 2, 14)
WINDOW = 10
SPAN = 8
PARTNERS = (PLANE - 1) + 2 * (NZ - 1) + 1 + 2

F32 = jnp.float32
BF16 = jnp.bfloat16


def dot_nt(a, b):
    return lax.dot_general(a, b, (((1,), (1,)), ((), ())), preferred_element_type=F32)


def dot_nn(a, b):
    return lax.dot_general(a, b, (((1,), (0,)), ((), ())), preferred_element_type=F32)


def dot_tn(a, b):
    return lax.dot_general(a, b, (((0,), (0,)), ((), ())), preferred_element_type=F32)


def columns(head):
    return pl.ds(pl.multiple_of(head * HEAD, HEAD), HEAD)


def kernel(
    q_hbm, k_hbm, v_hbm, g_hbm, table_ref, ub_ref, vb_ref,
    att_ref, qg_ref, kg_ref, vg_ref, tg_ref, cg_ref, pg_ref,
    q_buf, g_buf, k_buf, v_buf, own_k, own_v, query_in, grad_in, stats, stats_out, stats_in, stats_rows,
    msg_f, tz, flat, table, tgrad_out, tgrad_in, parts, sib_in, half_out, half_in, fin,
    local_sem, own_sem, halo_s, halo_r, stat_s, stat_r, tz_s, tz_r, sib_s, sib_r,
    tab_s, tab_r, tg_s, tg_r, half_s, half_r, fin_s, fin_r,
):
    dp = lax.axis_index("dp")
    seq = lax.axis_index("seq")
    zl = dp // 2
    core = dp % 2
    other = 1 - core
    plane = seq // 2
    zh = seq % 2

    def remote(src, dst, ss, rs, to_dp, to_seq):
        return pltpu.make_async_remote_copy(
            src_ref=src, dst_ref=dst, send_sem=ss, recv_sem=rs,
            device_id={"dp": to_dp, "seq": to_seq}, device_id_type=pl.DeviceIdType.MESH,
        )

    def seq_at(step):
        return (seq + step + 32) % 32

    def plane_seq(p):
        return p * 2 + zh

    def turn(i, step):
        return (i + seq_at(step) // 2) % H

    load_q = pltpu.make_async_copy(q_hbm, q_buf, local_sem.at[0])
    load_g = pltpu.make_async_copy(g_hbm, g_buf, local_sem.at[1])

    def load_own(which):
        src, dst = ((k_hbm, k_buf), (v_hbm, v_buf))[which]
        return pltpu.make_async_copy(src, dst.at[pl.ds(MEM, SEG)], own_sem.at[which])

    barrier = pltpu.get_barrier_semaphore()

    def greet(to_dp, to_seq):
        pl.semaphore_signal(
            barrier, inc=1, device_id={"dp": to_dp, "seq": to_seq},
            device_id_type=pl.DeviceIdType.MESH,
        )

    greet(dp, seq_at(1))
    greet(dp, seq_at(-1))
    greet(zl * 2 + other, seq)

    @pl.loop(1, NZ)
    def _(p):
        for half in (0, 1):
            greet(((zl + p) % NZ) * 2 + core, plane * 2 + half)

    @pl.loop(1, PLANE)
    def _(p):
        greet(dp, plane_seq((plane + p) % PLANE))

    load_q.start()
    load_g.start()

    load_own(0).start()
    load_own(1).start()

    rows_in = table_ref[:, columns(plane)].astype(F32)
    for r in range(ROWS):
        msg_f[ROWS - 1 - r : ROWS - r, :] = rows_in[r : r + 1, :]
    msg_f[ROWS : ROWS + 1, :] = ub_ref[...].astype(F32)
    msg_f[ROWS + 1 : ROWS + 2, :] = vb_ref[...].astype(F32)
    msg_f[ROWS + 2 : MSG, :] = jnp.zeros((MSG - ROWS - 2, HEAD), F32)
    tz[core, zl] = msg_f[...].astype(BF16)

    stats[...] = jnp.zeros_like(stats)

    pl.semaphore_wait(barrier, PARTNERS)

    def table_z(target, sem):
        return remote(tz.at[core, zl], tz.at[core, zl], tz_s.at[target], tz_r.at[sem], target * 2 + core, seq)

    @pl.loop(1, NZ)
    def _(p):
        table_z((zl + p) % NZ, zl).start()

    def halo(h, which, step):
        src = (k_hbm, v_hbm, q_hbm, g_hbm)[which]
        dst = (k_buf, v_buf, query_in, grad_in)[which]
        low, target = (MEM - step * SEG, seq_at(step)) if which < 2 else ((step - 1) * SEG, seq_at(-step))
        return remote(
            src.at[:, columns(h)], dst.at[pl.ds(low, SEG), columns(h)],
            halo_s.at[which, step - 1, h], halo_r.at[which, step - 1, h], dp, target,
        )

    @pl.loop(1, NZ)
    def _(p):
        source = (zl + p) % NZ
        remote(tz.at[core, zl], tz.at[core, source], tz_s.at[source], tz_r.at[source], source * 2 + core, seq).wait_recv()

    sib_table = remote(tz.at[core], tz.at[core], sib_s.at[0], sib_r.at[0], zl * 2 + other, seq)
    sib_table.start()

    def beside(group, which):
        src = (k_hbm, v_hbm, q_hbm, g_hbm)[which]
        dst = (k_buf, v_buf, query_in, grad_in)[which]
        low, target = (0, seq_at(2)) if which < 2 else (SEG, seq_at(-2))
        at = pl.ds(pl.multiple_of(group * SPAN * HEAD, HEAD), SPAN * HEAD)
        return remote(
            src.at[:, at], dst.at[pl.ds(low, SEG), at],
            halo_s.at[which, 1, group], halo_r.at[which, 1, group], dp, target,
        )

    def feed(n):
        @pl.when(n < H)
        def _():
            for which in (0, 1):
                halo(turn(n, 1), which, 1).start()

        @pl.when((n >= H) & (n < 2 * H))
        def _():
            for which in (2, 3):
                halo(turn(n - H, -1), which, 1).start()

    @pl.loop(0, WINDOW)
    def _(n):
        feed(n)

    remote(tz.at[core], tz.at[other], sib_s.at[0], sib_r.at[0], zl * 2 + other, seq).wait_recv()

    for d in range(DP):
        low = REL - ROWS * (d + 1)
        flat[low : low + ROWS, :] = tz[d % 2, d // 2].astype(F32)[:ROWS]
    table[plane] = flat[...].astype(BF16)

    def table_plane(p, slot, target):
        return remote(table.at[plane], table.at[slot], tab_s.at[p], tab_r.at[slot], dp, plane_seq(target))

    @pl.loop(1, PLANE)
    def _(p):
        table_plane(p, plane, (plane - p + PLANE) % PLANE).start()

    @pl.loop(0, H // SPAN)
    def _(i):
        for which in (0, 1):
            beside((turn(0, 2) // SPAN + i) % (H // SPAN), which).start()

    @pl.loop(0, H // SPAN)
    def _(i):
        for which in (2, 3):
            beside((turn(0, -2) // SPAN + i) % (H // SPAN), which).start()

    load_q.wait()
    load_g.wait()

    query_index = lax.broadcasted_iota(jnp.int32, (SEG, REL), 0)
    column_index = lax.broadcasted_iota(jnp.int32, (SEG, REL), 1)
    factor = HEAD ** (-0.5)
    mirror = (
        lax.broadcasted_iota(jnp.int32, (SEG, SEG), 0) + lax.broadcasted_iota(jnp.int32, (SEG, SEG), 1) == SEG - 1
    ).astype(F32).astype(BF16)

    lane_index = lax.broadcasted_iota(jnp.int32, (SEG, HEAD), 1)
    half_heads = H // 2

    def with_biases(query, h):
        biases = tz[h % 2, h // 2].astype(F32)
        query = query.astype(F32)
        return (query + biases[ROWS : ROWS + 1]).astype(BF16), (query + biases[ROWS + 1 : ROWS + 2]).astype(BF16)

    def send_stats(group, step):
        rows = pl.ds(group * STAT * half_heads, STAT * half_heads)
        return remote(
            stats_out.at[rows], stats_in.at[step - 1, rows],
            stat_s.at[group, step - 1], stat_r.at[group, step - 1], dp, seq_at(-step),
        )

    def send_tgrad(h):
        return remote(tgrad_out.at[h], tgrad_in.at[plane], tg_s.at[h], tg_r.at[plane], dp, plane_seq(h))

    @pl.loop(0, H)
    def _(i):
        h = turn(i, 0)

        @pl.when(h != plane)
        def _():
            table_plane(0, h, h).wait_recv()

        @pl.when(i == 0)
        def _():
            load_own(0).wait()
            load_own(1).wait()

        group = h // SPAN

        @pl.when((i == 0) | ((h % SPAN == 0) & (group != plane // SPAN)))
        def _():
            for which in (0, 1):
                beside(group, which).wait_recv()

        for which in (0, 1):
            halo(h, which, 1).wait_recv()
        feed(i + WINDOW)
        at = columns(h)
        grad = g_buf[:, at]
        content_query, position_query = with_biases(q_buf[:, at], h)
        keys = k_buf[:, at]
        values = v_buf[:, at]
        rows = table[h]
        positional = pltpu.roll(dot_nt(position_query, rows), REL - SEG + 1, 1, stride=1, stride_axis=0)
        scores = (dot_nt(content_query, keys) + positional) * factor
        allowed = (column_index <= query_index + MEM) & (column_index >= MEM - seq * SEG)
        scores = jnp.where(allowed, scores, -1e30)
        highest = jnp.max(scores, axis=1, keepdims=True)
        raised = jnp.where(allowed, jnp.exp(scores - highest), 0.0)
        inverse = 1.0 / jnp.sum(raised, axis=1, keepdims=True)
        weights = raised * inverse
        rounded = weights.astype(BF16)
        att_ref[:, at] = dot_nn(rounded, values).astype(BF16)
        grad_probs = dot_nt(grad, values)
        mean = jnp.sum(weights * grad_probs, axis=1, keepdims=True)
        grad_scores = (weights * (grad_probs - mean) * factor).astype(BF16)
        backwards = dot_nn(mirror, grad_scores)
        skewed = dot_nn(mirror, pltpu.roll(backwards, 0, 1, stride=1, stride_axis=0).astype(BF16)).astype(BF16)
        grad_content = dot_nn(grad_scores, keys)
        grad_position = dot_nn(skewed, rows)
        qg_ref[:, at] = (grad_content + grad_position).astype(BF16)
        own_k[h] = dot_tn(grad_scores[:, MEM:], content_query)
        own_v[h] = dot_tn(rounded[:, MEM:], grad)
        base = i * STAT
        stats[...] = jnp.where(lane_index == base, highest, jnp.where(
            lane_index == base + 1, inverse, jnp.where(lane_index == base + 2, mean, stats[...])))

        for group in (0, 1):
            @pl.when(i == half_heads * (group + 1) - 1)
            def _():
                flipped = stats[...].T
                rows = slice(group * STAT * half_heads, (group + 1) * STAT * half_heads)
                stats_out[rows] = flipped[rows]
                for step in (1, 2):
                    send_stats(group, step).start()

        tgrad_out[h, :REL] = dot_tn(skewed, position_query).astype(BF16)
        content_sum = jnp.sum(grad_content, axis=0, keepdims=True)
        position_sum = jnp.sum(grad_position, axis=0, keepdims=True)
        content_high = content_sum.astype(BF16).astype(F32)
        position_high = position_sum.astype(BF16).astype(F32)
        line = lax.broadcasted_iota(jnp.int32, (TGRAD - REL, HEAD), 0)
        sums = jnp.where(line == 0, content_high, jnp.where(line == 1, content_sum - content_high, jnp.where(
            line == 2, position_high, jnp.where(line == 3, position_sum - position_high, 0.0))))
        tgrad_out[h, REL:] = sums.astype(BF16)

        @pl.when(h != plane)
        def _():
            send_tgrad(h).start()

    sib_parts = remote(parts.at[other], sib_in, sib_s.at[1], sib_r.at[1], zl * 2 + other, seq)

    def send_half(half, target, slot):
        return remote(
            half_out.at[target], half_in.at[slot], half_s.at[half, target], half_r.at[slot],
            target * 2 + core, plane * 2 + half,
        )

    def along_z(act):
        act(1 - zh, zl)

        @pl.loop(1, NZ)
        def _(p):
            act(zh, (zl + p) % NZ)
            act(1 - zh, (zl + p) % NZ)

    def send_fin(p, slot, target):
        return remote(fin.at[plane], fin.at[slot], fin_s.at[p], fin_r.at[slot], dp, plane_seq(target))

    def take_stats(step, groups):
        for group in groups:
            send_stats(group, step).wait_recv()
        width = STAT * half_heads
        taken = [stats_in[step - 1, group * width : (group + 1) * width] for group in groups] * (3 - len(groups))
        taken.append(jnp.zeros((SEG - 2 * width, HEAD), F32))
        stats_rows[step - 1] = jnp.concatenate(taken, axis=0).T

    def later_part(h, step):
        content_query, position_query = with_biases(query_in[(step - 1) * SEG : step * SEG, columns(h)], h)
        grad = grad_in[(step - 1) * SEG : step * SEG, columns(h)]
        rows = table[h, MEM - step * SEG : 2 * MEM - step * SEG]
        positional = pltpu.roll(dot_nt(position_query, rows), SEG + 1, 1, stride=1, stride_axis=0)[:, :SEG]
        scores = (dot_nt(content_query, k_buf[MEM:, columns(h)]) + positional) * factor
        base = ((h - seq_at(step) // 2 + H) % H) * STAT
        column = lambda at: jnp.sum(
            jnp.where(lane_index == base + at, stats_rows[step - 1], 0.0), axis=1, keepdims=True)
        weights = jnp.where(
            lane_index < (32 - step - seq) * HEAD, jnp.exp(scores - column(0)) * column(1), 0.0)
        grad_probs = dot_nt(grad, v_buf[MEM:, columns(h)])
        grad_scores = (weights * (grad_probs - column(2)) * factor).astype(BF16)
        return dot_tn(grad_scores, content_query), dot_tn(weights.astype(BF16), grad)

    @pl.loop(0, H)
    def _(i):
        @pl.when(i == STAGES[0])
        def _():
            flat[...] = tgrad_out[plane, :REL].astype(F32)
            msg_f[0:16, :] = tgrad_out[plane, REL:].astype(F32)

            @pl.loop(1, PLANE)
            def _(p):
                source = (plane + p) % PLANE
                remote(tgrad_out.at[source], tgrad_in.at[source], tg_s.at[source], tg_r.at[source], dp, plane_seq(source)).wait_recv()
                flat[...] += tgrad_in[source, :REL].astype(F32)
                msg_f[0:16, :] += tgrad_in[source, REL:].astype(F32)

            tail_rows = msg_f[0:16, :]
            content_total = tail_rows[0:1] + tail_rows[1:2]
            position_total = tail_rows[2:3] + tail_rows[3:4]
            line = lax.broadcasted_iota(jnp.int32, (MSG - ROWS, HEAD), 0)
            sums = jnp.where(line == 0, content_total, jnp.where(line == 1, position_total, 0.0))
            for d in range(DP):
                low = REL - ROWS * (d + 1)
                parts[d % 2, d // 2, :ROWS] = flat[low : low + ROWS, :]
                parts[d % 2, d // 2, ROWS:] = sums
            sib_parts.start()

        @pl.when(i == STAGES[1])
        def _():
            sib_parts.wait_recv()
            parts[core] += sib_in[...]
            low = lax.broadcasted_iota(jnp.int32, (MSG, HEAD), 0)

            @pl.loop(0, NZ)
            def _(p):
                block = parts[core, p]
                rest = block - block.astype(BF16).astype(F32)
                block = jnp.where(low == ROWS + 2, rest[ROWS : ROWS + 1], jnp.where(
                    low == ROWS + 3, rest[ROWS + 1 : ROWS + 2], block))
                half_out[p] = block.astype(BF16)

            along_z(lambda half, target: send_half(half, target, zh * NZ + zl).start())

        @pl.when(i == STAGES[2])
        def _():
            fin[plane] = half_out[zl].astype(F32)

            def add(half, source):
                slot = half * NZ + source
                remote(half_out.at[source], half_in.at[slot], half_s.at[half, source], half_r.at[slot],
                       source * 2 + core, plane * 2 + half).wait_recv()
                fin[plane] += half_in[slot].astype(F32)

            along_z(add)
            total = fin[plane]
            for r in range(ROWS):
                fin[plane, r : r + 1] = total[ROWS - 1 - r : ROWS - r]

            @pl.loop(1, PLANE)
            def _(p):
                send_fin(p, plane, (plane + p) % PLANE).start()

        h = turn(i, 1)
        @pl.when(i == 0)
        def _():
            take_stats(1, (0,))
            take_stats(2, (0, 1))

            @pl.loop(0, H // SPAN)
            def _(group):
                for which in (2, 3):
                    beside(group, which).wait_recv()

        @pl.when(i == half_heads)
        def _():
            take_stats(1, (1,))

        for which in (2, 3):
            halo(h, which, 1).wait_recv()
        feed(i + H + WINDOW)
        key_near, value_near = later_part(h, 1)
        key_far, value_far = later_part(h, 2)
        at = columns(h)
        kg_ref[:, at] = (own_k[h] + key_near + key_far).astype(BF16)
        vg_ref[:, at] = (own_v[h] + value_near + value_far).astype(BF16)

    @pl.loop(1, PLANE)
    def _(p):
        source = (plane + p) % PLANE
        send_fin(p, source, source).wait_recv()

    @pl.loop(0, H)
    def _(h):
        tg_ref[:, columns(h)] = fin[h, :ROWS]

    mine = fin[dp]
    cg_ref[...] = mine[ROWS : ROWS + 1] + mine[ROWS + 2 : ROWS + 3]
    pg_ref[...] = mine[ROWS + 1 : ROWS + 2] + mine[ROWS + 3 : ROWS + 4]

    sib_table.wait_send()
    sib_parts.wait_send()

    @pl.loop(1, NZ)
    def _(p):
        target = (zl + p) % NZ
        table_z(target, zl).wait_send()

    @pl.loop(1, PLANE)
    def _(p):
        target = (plane + p) % PLANE
        table_plane(p, plane, (plane - p + PLANE) % PLANE).wait_send()
        send_fin(p, plane, target).wait_send()
        send_tgrad(target).wait_send()

    along_z(lambda half, target: send_half(half, target, zh * NZ + zl).wait_send())
    for step in (1, 2):
        for group in (0, 1):
            send_stats(group, step).wait_send()

    @pl.loop(0, H)
    def _(h):
        for which in range(4):
            halo(h, which, 1).wait_send()

    @pl.loop(0, H // SPAN)
    def _(group):
        for which in range(4):
            beside(group, which).wait_send()


def local(queries, keys, values, position_keys, content_bias, position_bias, out_grad):
    hbm = pl.BlockSpec(memory_space=pltpu.HBM)
    vmem = pl.BlockSpec(memory_space=pltpu.VMEM)
    block = jax.ShapeDtypeStruct((SEG, HD), BF16)
    line = jax.ShapeDtypeStruct((1, HEAD), F32)
    dma = pltpu.SemaphoreType.DMA
    heads = lambda rows, dtype: pltpu.VMEM((H, rows, HEAD), dtype)
    attended, query_grad, key_grad, value_grad, table_grad, content_grad, position_grad = pl.pallas_call(
        kernel,
        out_shape=(block, block, block, block, jax.ShapeDtypeStruct((ROWS, HD), F32), line, line),
        in_specs=[hbm] * 4 + [vmem] * 3,
        out_specs=(vmem,) * 7,
        scratch_shapes=[
            pltpu.VMEM((SEG, HD), BF16),
            pltpu.VMEM((SEG, HD), BF16),
            pltpu.VMEM((REL, HD), BF16),
            pltpu.VMEM((REL, HD), BF16),
            heads(SEG, F32),
            heads(SEG, F32),
            pltpu.VMEM((MEM, HD), BF16),
            pltpu.VMEM((MEM, HD), BF16),
            pltpu.VMEM((SEG, HEAD), F32),
            pltpu.VMEM((STAT * H, HEAD), F32),
            pltpu.VMEM((2, STAT * H, HEAD), F32),
            pltpu.VMEM((2, SEG, HEAD), F32),
            pltpu.VMEM((MSG, HEAD), F32),
            pltpu.VMEM((2, NZ, MSG, HEAD), BF16),
            pltpu.VMEM((REL, HEAD), F32),
            heads(REL, BF16),
            heads(TGRAD, BF16),
            heads(TGRAD, BF16),
            pltpu.VMEM((2, NZ, MSG, HEAD), F32),
            pltpu.VMEM((NZ, MSG, HEAD), F32),
            pltpu.VMEM((NZ, MSG, HEAD), BF16),
            pltpu.VMEM((2 * NZ, MSG, HEAD), BF16),
            heads(MSG, F32),
            dma((2,)),
            dma((2,)),
            dma((4, 2, H)),
            dma((4, 2, H)),
            dma((2, 2)),
            dma((2, 2)),
            dma((NZ,)),
            dma((NZ,)),
            dma((2,)),
            dma((2,)),
            dma((PLANE,)),
            dma((PLANE,)),
            dma((H,)),
            dma((PLANE,)),
            dma((2, NZ)),
            dma((2 * NZ,)),
            dma((PLANE,)),
            dma((PLANE,)),
        ],
        compiler_params=pltpu.CompilerParams(
            collective_id=0, has_side_effects=True, vmem_limit_bytes=52 * 2**20
        ),
    )(
        queries[0], keys[0], values[0], out_grad[0],
        position_keys, content_bias[None], position_bias[None],
    )
    return (
        attended[None],
        query_grad[None],
        key_grad[None],
        value_grad[None],
        table_grad,
        content_grad[0],
        position_grad[0],
    )


def solution(mesh):
    placed = (
        P("dp", "seq", None),
        P("dp", "seq", None),
        P("dp", "seq", None),
        P("dp", None),
        P("dp"),
        P("dp"),
        P("dp", "seq", None),
    )
    return jax.shard_map(
        local,
        mesh=mesh,
        in_specs=placed,
        out_specs=(
            P("dp", "seq", None),
            P("dp", "seq", None),
            P("dp", "seq", None),
            P("dp", "seq", None),
            P("dp", None),
            P("dp"),
            P("dp"),
        ),
        check_vma=False,
    )
```
